32 devices in a mesh: groups: 2 (over x), dp: 16 (over z, y, core).
Axes of the slice: x: 2, y: 2, z: 4, core: 2. Of those that a mesh axis runs over, the one named last changes fastest.
Arguments:
- hidden: bfloat16 [32, 8192], P(('groups', 'dp')), parts along dimension 0, may hold values from -6 to 6
- query_weight: bfloat16 [8192, 8192], P(None, 'dp'), may hold values from -0.0625 to 0.0625
- output_weight: bfloat16 [8192, 8192], P(None, 'dp'), may hold values from -0.0625 to 0.0625
- adapter_down: bfloat16 [64, 2, 8192, 64], P('dp'), may hold values from -0.0625 to 0.0625
- adapter_up: bfloat16 [64, 2, 64, 8192], P('dp'), may hold values from -0.75 to 0.75
- kv_cache: bfloat16 [32, 2, 512, 1024], P(('groups', 'dp')), parts along dimension 0
- cache_lengths: int32 [32], P(('groups', 'dp')), parts along dimension 0, may hold values from 1 to 512, as said below
- row_variant: int32 [32], P('groups'), parts along dimension 0, may hold values from 0 to 63
- variant_slot: int32 [64], replicated, may hold values from 0 to 63, as said below
Outputs:
- attended: bfloat16 [32, 8192], P(('groups', 'dp')), parts along dimension 0
The draws below stay inside these ranges and needn't reach their ends.
There are 2 independent parts, one for each index of `groups`. The reference program is written for one: setup_inputs(seed, part) draws one part's arguments, and reference() takes and returns one part's arrays. A program takes and returns all parts, laid end to end along the dimension named above; an argument that names none is the same for every part. Nothing has to cross between parts.
Inputs may be any that keep to these rules, and one draw needn't show every extreme that they name: `cache_lengths`: some row's length is 512. `variant_slot`: distinct slots; slot s is held by index s // 4 of dp. Slot 63 is always used.
All inputs are finite; a program needn't handle non-finite values.
Results may differ from the reference program's by a relative error of at most 0.02.
The reference program's roundings to bfloat16 on the way count: a program that leaves them out, or rounds other values in their place, can miss the bound.
Values may be sent and summed in bfloat16 or wider, within the bound.
A program may use at most 192 MiB of HBM per device.

```python
import math
import jax
import jax.numpy as jnp
from jax import lax

HEADS = 64
KVH = 8
HDIM = 128
RANK = 64
VARIANTS = 64
CACHE = 512
D = 8192
ROWS = 16
STORE = 64


def draw_kv_cache(key, part):
    key = jax.random.fold_in(key, 3)
    base_key = jax.random.fold_in(key, 0)
    entries = jax.random.normal(base_key, (ROWS, 2, CACHE, KVH * HDIM), jnp.float32)
    factor = jnp.array([1.5, 1.0], jnp.float32).reshape(1, 2, 1, 1)
    return (entries * factor).astype(jnp.bfloat16)


def draw_cache_lengths(key, part):
    key = jax.random.fold_in(key, 1)
    lengths = jax.random.randint(key, (ROWS,), 1, CACHE + 1, jnp.int32)
    return lengths.at[0].set(CACHE)


def draw_variant_slot(key, part):
    key = jax.random.fold_in(key, 2)
    shuffled = jax.random.permutation(key, STORE)[:VARIANTS].astype(jnp.int32)
    present = jnp.any(shuffled == STORE - 1)
    return jnp.where(present, shuffled, shuffled.at[0].set(STORE - 1))


def plant(values, rng, smallest, largest):
    longest = values.shape.index(max(values.shape))
    spots = []
    for shift in (0, 1):
        where = [jax.random.randint(jax.random.fold_in(rng, axis), (), 0, length) for axis, length in enumerate(values.shape)]
        where[longest] = (where[longest] + shift) % values.shape[longest]
        spots.append(tuple(where))
    return values.at[spots[0]].set(smallest).at[spots[1]].set(largest)


def shard_levels(own_key, extent, cuts, least, top_value):
    factor_of = 1.0
    for axis_at, blocks in cuts:
        heights = jax.random.uniform(jax.random.fold_in(jax.random.fold_in(own_key, 6), axis_at), (blocks,), jnp.float32, least / len(cuts), top_value / len(cuts))
        factor_of = factor_of * jnp.repeat(jnp.exp(heights), extent[axis_at] // blocks).reshape((-1,) + (1,) * (len(extent) - 1 - axis_at))
    return factor_of


def centred(key, extent, deviation, bound, pieces=(), kind=jnp.bfloat16):
    values = deviation * jax.random.normal(key, extent, jnp.float32)
    if pieces:
        values = values * shard_levels(key, extent, pieces, -0.22, 0.18)
    return jnp.clip(values, -bound, bound).astype(kind)


def setup_inputs(seed: int = 0, part: int = 0) -> dict:
    seeds = jax.random.split(jax.random.key(seed), 10)
    own_keys = jax.random.split(jax.random.fold_in(seeds[9], part), 10)
    return {
        "hidden": centred(own_keys[0], (ROWS, D), 1.0, 6.0, ((0, 16),)),
        "query_weight": centred(seeds[1], (D, D), D ** -0.5, 0.0625, ((1, 16),)),
        "output_weight": centred(seeds[2], (D, D), D ** -0.5, 0.0625, ((1, 16),)),
        "adapter_down": centred(seeds[3], (STORE, 2, D, RANK), D ** -0.5, 0.0625, ((0, 16),)),
        "adapter_up": centred(seeds[4], (STORE, 2, RANK, D), RANK ** -0.5, 0.75, ((0, 16),)),
        "kv_cache": draw_kv_cache(jax.random.fold_in(jax.random.fold_in(seeds[9], part), 71), part),
        "cache_lengths": draw_cache_lengths(jax.random.fold_in(jax.random.fold_in(seeds[9], part), 71), part),
        "row_variant": plant(jax.random.randint(own_keys[7], (ROWS,), 0, VARIANTS), jax.random.fold_in(own_keys[7], 1), 0, VARIANTS - 1).astype(jnp.int32),
        "variant_slot": draw_variant_slot(jax.random.fold_in(seeds[9], 71), part),
    }


def project(row_block, weight, target, adapter_down, adapter_up, row_slot):
    base_part = jnp.dot(row_block, weight, preferred_element_type=jnp.float32).astype(jnp.bfloat16)

    def adapt_single(record):
        single, slot_index = record
        reduced = jnp.dot(single, adapter_down[slot_index, target], preferred_element_type=jnp.float32).astype(jnp.bfloat16)
        return jnp.dot(reduced, adapter_up[slot_index, target], preferred_element_type=jnp.float32).astype(jnp.bfloat16)
    deltas = lax.map(adapt_single, (row_block, row_slot))
    return (base_part.astype(jnp.float32) + deltas.astype(jnp.float32)).astype(jnp.bfloat16)

def reference(hidden, query_weight, output_weight, adapter_down, adapter_up, kv_cache, cache_lengths, row_variant, variant_slot):
    row_slot = variant_slot[row_variant].astype(jnp.int32)
    queries = project(hidden, query_weight, 0, adapter_down, adapter_up, row_slot)
    scaling = 1.0 / math.sqrt(HDIM)

    def attend(record):
        query_row, cache_row, length = record
        grouped = query_row.astype(jnp.float32).reshape(KVH, HEADS // KVH, HDIM)
        key_rows = cache_row[0].astype(jnp.float32).reshape(-1, KVH, HDIM)
        value_rows = cache_row[1].astype(jnp.float32).reshape(-1, KVH, HDIM)
        scores = jnp.einsum('kgd,ckd->kgc', grouped, key_rows) * scaling
        visible = jnp.arange(key_rows.shape[0], dtype=jnp.int32) < length
        masked = jnp.where(visible, scores, -1e+30)
        highest = lax.optimization_barrier(jnp.max(masked, axis=-1, keepdims=True))
        expon = jnp.where(visible, jnp.exp(masked - highest), 0.0)
        probs = (expon / lax.optimization_barrier(jnp.sum(expon, axis=-1, keepdims=True))).astype(jnp.bfloat16)
        mixed = jnp.einsum('kgc,ckd->kgd', probs.astype(jnp.float32), value_rows)
        return mixed.astype(jnp.bfloat16).reshape(-1)
    mixed = lax.map(attend, (queries, kv_cache, cache_lengths))
    return project(mixed, output_weight, 1, adapter_down, adapter_up, row_slot)
```

```python
import functools
import math

import jax
import jax.numpy as jnp
from jax import lax
from jax.experimental import pallas as pl
from jax.experimental.pallas import tpu as pltpu
from jax.sharding import PartitionSpec as P

HEADS = 64
KVH = 8
HDIM = 128
GROUP = HEADS // KVH
F32 = jnp.float32
BF16 = jnp.bfloat16
SCALING = 1.0 / math.sqrt(HDIM)
MIB = 1 << 20
NN = (((1,), (0,)), ((), ()))
NT = (((1,), (1,)), ((), ()))


def attention_kernel(
    n,
    variant_ref,
    slots_ref,
    length_ref,
    hidden_ref,
    wq_hbm,
    wo_hbm,
    down_hbm,
    up_hbm,
    kv_hbm,
    out_ref,
    weight,
    down,
    up,
    kv,
    gathered,
    wide,
    rows,
    row32,
    own_delta,
    sibling_delta,
    pair_delta,
    delta_in,
    base_out,
    base_in,
    local_sem,
    gather_send,
    gather_recv,
    pair_send,
    pair_recv,
    delta_send,
    delta_recv,
    base_send,
    base_recv,
):
    chips = n // 2
    deep = chips // 2
    owned = down_hbm.shape[0]
    rank = down_hbm.shape[2]
    width = down_hbm.shape[3]
    cols = wq_hbm.shape[1]
    blocks = cols // HDIM
    me = lax.axis_index("dp")
    core = lax.rem(me, 2)
    chip = lax.div(me, 2)
    y = lax.rem(chip, 2)
    z = lax.div(chip, 2)
    here = core * chips + chip

    def copy_to(src, dst, send, recv, dev):
        return pltpu.make_async_remote_copy(
            src_ref=src,
            dst_ref=dst,
            send_sem=send,
            recv_sem=recv,
            device_id={"dp": dev},
            device_id_type=pl.DeviceIdType.MESH,
        )

    depth = width // WPARTS
    loads = {}
    count = 0

    def load(name, src, dst):
        nonlocal count
        copy = pltpu.make_async_copy(src, dst, local_sem.at[count])
        count += 1
        copy.start()
        loads.setdefault(name, []).append(copy)

    for phase, w_hbm in ((0, wq_hbm), (1, wo_hbm)):
        for s in range(owned):
            load(("down", phase), down_hbm.at[s, phase], down.at[phase, pl.ds(s * rank, rank)])
        for s in range(owned):
            load(("up", phase), up_hbm.at[s, phase], up.at[phase, pl.ds(s * rank, rank)])
        for part in range(WPARTS):
            cut = pl.ds(part * depth, depth)
            load(("weight", phase, part), w_hbm.at[cut], weight.at[phase, cut])
        if phase == 0:
            load("kv", kv_hbm.at[0], kv)

    def loaded(name):
        for copy in loads[name]:
            copy.wait()

    for c in range(HEADS):
        row32[pl.ds(c, 1), :] = hidden_ref[:, c * HDIM : (c + 1) * HDIM].astype(F32)

    barrier = pltpu.get_barrier_semaphore()
    for k in range(1, n):
        pl.semaphore_signal(
            barrier,
            inc=1,
            device_id={"dp": lax.rem(me + k, n)},
            device_id_type=pl.DeviceIdType.MESH,
        )

    place = lax.broadcasted_iota(jnp.int32, (n, owned * rank), 0)
    lane_slot = me * owned + lax.div(
        lax.broadcasted_iota(jnp.int32, (n, owned * rank), 1), rank
    )
    row_slot = jnp.zeros((n, owned * rank), jnp.int32)
    for p in range(n):
        row = (p % chips) * 2 + p // chips
        row_slot = jnp.where(place == p, slots_ref[variant_ref[row]], row_slot)
    mine = row_slot == lane_slot

    pl.semaphore_wait(barrier, n - 1)

    def block(ref, phase, p):
        return ref.at[phase, pl.ds(pl.multiple_of(p * HEADS, HEADS), HEADS)]

    def project(phase):
        sibling = me + 1 - 2 * core
        across = (z * 2 + 1 - y) * 2 + core
        waits = []

        def send_row(p, dev, s):
            ref = block(gathered, phase, p)
            copy = copy_to(ref, ref, gather_send.at[phase, s], gather_recv.at[phase, p], dev)
            copy.start()
            waits.append(copy)

        def arrived(p):
            ref = block(gathered, phase, p)
            copy_to(ref, ref, gather_send.at[phase, 0], gather_recv.at[phase, p], me).wait_recv()

        gathered[phase, pl.ds(pl.multiple_of(here * HEADS, HEADS), HEADS), :] = row32[
            ...
        ].astype(BF16)
        s = 0
        for k in range(1, deep):
            zz = lax.rem(z + k, deep)
            send_row(here, (zz * 2 + y) * 2 + core, s)
            s += 1
        send_row(here, across, s)
        send_row(here, sibling, s + 1)
        s += 2
        for k in range(1, deep):
            zz = lax.rem(z + deep - k, deep)
            p = core * chips + zz * 2 + y
            arrived(p)
            send_row(p, across, s)
            send_row(p, sibling, s + 1)
            s += 2
        for k in range(deep):
            zz = lax.rem(z + deep - k, deep)
            p = core * chips + zz * 2 + 1 - y
            arrived(p)
            send_row(p, sibling, s)
            s += 1
        for k in range(chips):
            arrived((1 - core) * chips + k)

        wide[...] = gathered[phase].astype(F32)
        for c in range(HEADS):
            rows[:, c * HDIM : (c + 1) * HDIM] = wide[pl.ds(c, n, stride=HEADS), :].astype(BF16)

        loaded(("down", phase))

        def lower(k, acc):
            cut = pl.ds(pl.multiple_of(k * KSTEP, KSTEP), KSTEP)
            return acc + lax.dot_general(
                rows[:, cut], down[phase, :, cut], NT, preferred_element_type=F32
            )

        low = lax.fori_loop(0, width // KSTEP, lower, jnp.zeros((n, owned * rank), F32))
        codes = jnp.where(mine, low, 0.0).astype(BF16)
        loaded(("up", phase))

        def raise_(k, carry):
            cut = pl.ds(pl.multiple_of(k * NSTEP, NSTEP), NSTEP)
            term = lax.dot_general(codes, up[phase, :, cut], NN, preferred_element_type=F32)
            for j in range(NSTEP // HDIM):
                wide[pl.ds(k * (NSTEP // HDIM) + j, n, stride=HEADS), :] = term[
                    :, j * HDIM : (j + 1) * HDIM
                ]
            return carry

        lax.fori_loop(0, width // NSTEP, raise_, 0)
        own_delta[phase] = wide[...].astype(BF16)
        half = chips * HEADS
        to_pair = copy_to(
            own_delta.at[phase, pl.ds(pl.multiple_of((1 - core) * half, half), half)],
            sibling_delta.at[phase],
            pair_send.at[phase],
            pair_recv.at[phase],
            sibling,
        )
        to_pair.start()

        def base_part(part, acc):
            loaded(("weight", phase, part))

            def step(k, acc):
                cut = pl.ds(pl.multiple_of(part * depth + k * KSTEP, KSTEP), KSTEP)
                return acc + lax.dot_general(
                    rows[:, cut], weight[phase, cut, :], NN, preferred_element_type=F32
                )

            return lax.fori_loop(0, depth // KSTEP, step, acc)

        acc = base_part(0, jnp.zeros((n, cols), F32))

        to_pair.wait_recv()
        pair_delta[phase] = (
            own_delta[phase, pl.ds(pl.multiple_of(core * half, half), half), :].astype(F32)
            + sibling_delta[phase].astype(F32)
        ).astype(BF16)
        for k in range(1, chips):
            other = lax.rem(chip + k, chips)
            copy = copy_to(
                block(pair_delta, phase, other),
                block(delta_in, phase, chip),
                delta_send.at[phase, k],
                delta_recv.at[phase, chip],
                other * 2 + core,
            )
            copy.start()
            waits.append(copy)

        for part in range(1, WPARTS):
            acc = base_part(part, acc)
        acc = acc.astype(BF16).astype(F32)
        for j in range(blocks):
            base_out[phase, pl.ds(j, n, stride=8), :] = acc[:, j * HDIM : (j + 1) * HDIM]

        def part_of(ref, p):
            return ref.at[phase, pl.ds(pl.multiple_of(p * 8, 8), 8)]

        for k in range(1, n):
            dev = lax.rem(me + k, n)
            p = lax.rem(dev, 2) * chips + lax.div(dev, 2)
            copy = copy_to(
                part_of(base_out, p),
                part_of(base_in, me),
                base_send.at[phase, k],
                base_recv.at[phase, me],
                dev,
            )
            copy.start()
            waits.append(copy)
        base_in[phase, pl.ds(pl.multiple_of(me * 8, 8), 8), :] = base_out[
            phase, pl.ds(pl.multiple_of(here * 8, 8), 8), :
        ]

        total = pair_delta[
            phase, pl.ds(pl.multiple_of(chip * HEADS, HEADS), HEADS), :
        ].astype(F32)
        for k in range(1, chips):
            other = lax.rem(chip + chips - k, chips)
            ref = block(delta_in, phase, other)
            copy_to(
                ref, ref, delta_send.at[phase, 0], delta_recv.at[phase, other], me
            ).wait_recv()
            total = total + delta_in[
                phase, pl.ds(pl.multiple_of(other * HEADS, HEADS), HEADS), :
            ].astype(F32)
        for k in range(1, n):
            src = lax.rem(me + n - k, n)
            ref = part_of(base_in, src)
            copy_to(ref, ref, base_send.at[phase, 0], base_recv.at[phase, src], me).wait_recv()
        for src in range(n):
            row32[pl.ds(src * blocks, blocks), :] = base_in[phase, pl.ds(src * 8, blocks), :]
        result = (row32[...] + total).astype(BF16)
        to_pair.wait_send()
        for copy in waits:
            copy.wait_send()
        return result

    row32[...] = project(0).astype(F32)

    loaded("kv")
    cache_len = kv.shape[1]
    length = length_ref[0]
    scores = []
    for g in range(KVH):
        q = row32[pl.ds(g * GROUP, GROUP), :].astype(BF16)
        scores.append(
            lax.dot_general(
                q, kv[0, :, g * HDIM : (g + 1) * HDIM], NT, preferred_element_type=F32
            )
        )
    scores = jnp.concatenate(scores, axis=0) * SCALING
    visible = lax.broadcasted_iota(jnp.int32, (HEADS, cache_len), 1) < length
    masked = jnp.where(visible, scores, -1e30)
    highest = jnp.max(masked, axis=-1, keepdims=True)
    expon = jnp.where(visible, jnp.exp(masked - highest), 0.0)
    probs = expon / jnp.sum(expon, axis=-1, keepdims=True)
    for g in range(KVH):
        row32[pl.ds(g * GROUP, GROUP), :] = lax.dot_general(
            probs[g * GROUP : (g + 1) * GROUP].astype(BF16),
            kv[1, :, g * HDIM : (g + 1) * HDIM],
            NN,
            preferred_element_type=F32,
        )

    out_ref[...] = project(1)


WPARTS = 4
KSTEP = 1024
NSTEP = 512


def fused_body(
    hidden,
    query_weight,
    output_weight,
    adapter_down,
    adapter_up,
    kv_cache,
    cache_lengths,
    row_variant,
    variant_slot,
):
    n = lax.axis_size("dp")
    width = hidden.shape[1]
    owned, _, _, rank = adapter_down.shape
    cols = query_weight.shape[1]
    chips = n // 2
    smem = pl.BlockSpec(memory_space=pltpu.SMEM)
    vmem = pl.BlockSpec(memory_space=pltpu.VMEM)
    anywhere = pl.BlockSpec(memory_space=pl.ANY)
    dma = pltpu.SemaphoreType.DMA
    weights = width * (2 * cols + 4 * owned * rank)
    macs = n * weights + 2 * HEADS * HDIM * kv_cache.shape[2]
    out = pl.pallas_call(
        functools.partial(attention_kernel, n),
        out_shape=jax.ShapeDtypeStruct((HEADS, HDIM), BF16),
        in_specs=[smem, smem, smem, vmem] + [anywhere] * 5,
        out_specs=vmem,
        scratch_shapes=[
            pltpu.VMEM((2, width, cols), BF16),
            pltpu.VMEM((2, owned * rank, width), BF16),
            pltpu.VMEM((2, owned * rank, width), BF16),
            pltpu.VMEM(kv_cache.shape[1:], BF16),
            pltpu.VMEM((2, n * HEADS, HDIM), BF16),
            pltpu.VMEM((n * HEADS, HDIM), F32),
            pltpu.VMEM((n, width), BF16),
            pltpu.VMEM((HEADS, HDIM), F32),
            pltpu.VMEM((2, n * HEADS, HDIM), BF16),
            pltpu.VMEM((2, chips * HEADS, HDIM), BF16),
            pltpu.VMEM((2, chips * HEADS, HDIM), BF16),
            pltpu.VMEM((2, chips * HEADS, HDIM), BF16),
            pltpu.VMEM((2, n * 8, HDIM), F32),
            pltpu.VMEM((2, n * 8, HDIM), F32),
            dma((4 * owned + 2 * WPARTS + 1,)),
            dma((2, n)),
            dma((2, n)),
            dma((2,)),
            dma((2,)),
            dma((2, chips)),
            dma((2, chips)),
            dma((2, n)),
            dma((2, n)),
        ],
        compiler_params=pltpu.CompilerParams(
            collective_id=0, has_side_effects=True, vmem_limit_bytes=52 * MIB
        ),
        cost_estimate=pl.CostEstimate(
            flops=2 * macs,
            bytes_accessed=2 * (weights + kv_cache.size),
            transcendentals=HEADS * kv_cache.shape[2],
        ),
        name="adapter_attention",
    )(
        row_variant,
        variant_slot,
        cache_lengths,
        hidden,
        query_weight,
        output_weight,
        jnp.swapaxes(adapter_down, 2, 3),
        adapter_up,
        kv_cache,
    )
    return out.reshape(1, width)


def fits(mesh, hidden, query_weight, adapter_down, kv_cache):
    n = mesh.shape["dp"]
    cols = query_weight.shape[1] // n
    width = hidden.shape[1]
    owned = adapter_down.shape[0] // n
    held = 4 * width * cols + 8 * owned * adapter_down.shape[3] * width
    held += 2 * kv_cache.size // kv_cache.shape[0]
    return (
        hidden.shape[0] == n * mesh.shape["groups"]
        and width == HEADS * HDIM
        and n % 16 == 0
        and n <= 32
        and cols % HDIM == 0
        and cols <= 8 * HDIM
        and held <= 40 * MIB
    )


def body(
    hidden,
    query_weight,
    output_weight,
    adapter_down,
    adapter_up,
    kv_cache,
    cache_lengths,
    row_variant,
    variant_slot,
):
    devices = lax.axis_size("dp")
    myself = lax.axis_index("dp")
    owned = adapter_down.shape[0]
    rank_size = adapter_down.shape[3]
    width = hidden.shape[1]
    rows_dev = hidden.shape[0]
    all_rows = rows_dev * devices
    row_slot = jnp.sum(
        jnp.where(
            row_variant[:, None] == jnp.arange(variant_slot.shape[0], dtype=jnp.int32)[None, :],
            variant_slot[None, :],
            0,
        ),
        axis=1,
    )
    my_slots = myself * owned + jnp.arange(owned, dtype=jnp.int32)

    def project(row_block, weight, target):
        col_count = weight.shape[1]
        shard_rows = lax.all_gather(row_block, "dp", axis=0, tiled=True)
        base_part = jnp.dot(shard_rows, weight, preferred_element_type=jnp.float32)
        lowered = jnp.einsum(
            "pd,sdr->psr", shard_rows, adapter_down[:, target], preferred_element_type=jnp.float32
        )
        owner_mask = (row_slot[:, None] == my_slots[None, :]).astype(jnp.float32)
        reduced = jnp.sum(lowered * owner_mask[:, :, None], axis=1)
        joined = jnp.concatenate([base_part, reduced], axis=1)
        base_cols = joined[:, :col_count].astype(jnp.bfloat16)
        reduced = joined[:, col_count:]
        codes = reduced.astype(jnp.bfloat16)
        picked = (row_slot[:, None] == my_slots[None, :]).astype(jnp.bfloat16)
        spread = (picked[:, :, None] * codes[:, None, :]).reshape(all_rows, owned * rank_size)
        deltas = jnp.dot(
            spread,
            adapter_up[:, target].reshape(owned * rank_size, width),
            preferred_element_type=jnp.float32,
        ).astype(jnp.bfloat16)
        arrived = lax.all_to_all(base_cols, "dp", split_axis=0, concat_axis=1, tiled=True)
        returned = lax.all_to_all(
            deltas.reshape(all_rows, 1, width), "dp", split_axis=0, concat_axis=1, tiled=True
        )
        summed = jnp.sum(returned, axis=1, dtype=jnp.float32)
        return (arrived.astype(jnp.float32) + summed).astype(jnp.bfloat16)

    queries = project(hidden, query_weight, 0)
    cache_len = kv_cache.shape[2]
    grouped = queries.reshape(rows_dev, KVH, HEADS // KVH, HDIM)
    key_rows = kv_cache[:, 0].reshape(rows_dev, cache_len, KVH, HDIM)
    value_rows = kv_cache[:, 1].reshape(rows_dev, cache_len, KVH, HDIM)
    scaling = 1.0 / math.sqrt(HDIM)
    scores = (
        jnp.einsum("rkgd,rckd->rkgc", grouped, key_rows, preferred_element_type=jnp.float32)
        * scaling
    )
    visible = (jnp.arange(cache_len, dtype=jnp.int32)[None, :] < cache_lengths[:, None])[
        :, None, None, :
    ]
    masked = jnp.where(visible, scores, -1e30)
    highest = jnp.max(masked, axis=-1, keepdims=True)
    expon = jnp.where(visible, jnp.exp(masked - highest), 0.0)
    probs = (expon / jnp.sum(expon, axis=-1, keepdims=True)).astype(jnp.bfloat16)
    mixed = jnp.einsum("rkgc,rckd->rkgd", probs, value_rows, preferred_element_type=jnp.float32)
    mixed = mixed.astype(jnp.bfloat16).reshape(rows_dev, width)
    return project(mixed, output_weight, 1)


def solution(mesh):
    in_specs = (
        P(("groups", "dp"), None),
        P(None, "dp"),
        P(None, "dp"),
        P("dp", None, None, None),
        P("dp", None, None, None),
        P(("groups", "dp"), None, None, None),
        P(("groups", "dp")),
        P("groups"),
        P(),
    )

    def run(*args):
        fused = fits(mesh, args[0], args[1], args[3], args[5])
        return jax.shard_map(
            fused_body if fused else body,
            mesh=mesh,
            in_specs=in_specs,
            out_specs=P(("groups", "dp"), None),
            check_vma=False,
        )(*args)

    return run
```

```python
import functools
import math

import jax
import jax.numpy as jnp
from jax import lax
from jax.experimental import pallas as pl
from jax.experimental.pallas import tpu as pltpu
from jax.sharding import PartitionSpec as P

HEADS = 64
KVH = 8
HDIM = 128
GROUP = HEADS // KVH
HALF = HEADS // 2
F32 = jnp.float32
BF16 = jnp.bfloat16
SCALING = 1.0 / math.sqrt(HDIM)
MIB = 1 << 20
NN = (((1,), (0,)), ((), ()))
NT = (((1,), (1,)), ((), ()))


def attention_kernel(
    n,
    variant_hbm,
    slots_hbm,
    length_hbm,
    hidden_hbm,
    wq_hbm,
    wo_hbm,
    down_hbm,
    up_hbm,
    kv_hbm,
    out_ref,
    variant_ref,
    slots_ref,
    length_ref,
    hidden_ref,
    weight,
    down,
    up,
    kv,
    gathered,
    wide,
    rows,
    row32,
    own_delta,
    sibling_delta,
    pair_delta,
    delta_in,
    base_out,
    base_in,
    local_sem,
    gather_send,
    gather_recv,
    pair_send,
    pair_recv,
    delta_send,
    delta_recv,
    base_send,
    base_recv,
):
    chips = n // 2
    owned = down_hbm.shape[0]
    rank = down_hbm.shape[2]
    width = down_hbm.shape[3]
    cols = wq_hbm.shape[1]
    blocks = cols // HDIM
    me = lax.axis_index("dp")
    core = lax.rem(me, 2)
    chip = lax.div(me, 2)
    here = core * chips + chip

    def copy_to(src, dst, send, recv, dev):
        return pltpu.make_async_remote_copy(
            src_ref=src,
            dst_ref=dst,
            send_sem=send,
            recv_sem=recv,
            device_id={"dp": dev},
            device_id_type=pl.DeviceIdType.MESH,
        )

    depth = width // WPARTS
    loads = {}
    count = 0

    def load(name, src, dst):
        nonlocal count
        copy = pltpu.make_async_copy(src, dst, local_sem.at[count])
        count += 1
        copy.start()
        loads.setdefault(name, []).append(copy)

    load("hidden", hidden_hbm, hidden_ref)
    load("variant", variant_hbm, variant_ref)
    load("slots", slots_hbm, slots_ref)
    load("length", length_hbm, length_ref)
    for phase, w_hbm in ((0, wq_hbm), (1, wo_hbm)):
        for s in range(owned):
            load(("down", phase), down_hbm.at[s, phase], down.at[phase, pl.ds(s * rank, rank)])
        for s in range(owned):
            load(("up", phase), up_hbm.at[s, phase], up.at[phase, pl.ds(s * rank, rank)])
        for part in range(WPARTS):
            cut = pl.ds(part * depth, depth)
            load(("weight", phase, part), w_hbm.at[cut], weight.at[phase, cut])
        if phase == 0:
            load("kv", kv_hbm.at[0], kv)

    def loaded(name):
        for copy in loads[name]:
            copy.wait()

    barrier = pltpu.get_barrier_semaphore()
    for k in range(1, n):
        pl.semaphore_signal(
            barrier,
            inc=1,
            device_id={"dp": lax.rem(me + k, n)},
            device_id_type=pl.DeviceIdType.MESH,
        )

    loaded("hidden")
    for c in range(HEADS):
        row32[pl.ds(c, 1), :] = hidden_ref[:, c * HDIM : (c + 1) * HDIM].astype(F32)

    loaded("variant")
    loaded("slots")
    loaded("length")

    place = lax.broadcasted_iota(jnp.int32, (n, owned * rank), 0)
    lane_slot = me * owned + lax.div(
        lax.broadcasted_iota(jnp.int32, (n, owned * rank), 1), rank
    )
    row_slot = jnp.zeros((n, owned * rank), jnp.int32)
    for p in range(n):
        row = (p % chips) * 2 + p // chips
        row_slot = jnp.where(place == p, slots_ref[variant_ref[row]], row_slot)
    mine = row_slot == lane_slot

    pl.semaphore_wait(barrier, n - 1)

    def block(ref, phase, p):
        return ref.at[phase, pl.ds(pl.multiple_of(p * HEADS, HEADS), HEADS)]

    def project(phase):
        sibling = me + 1 - 2 * core
        waits = []

        def send_row(p, dev, s):
            ref = block(gathered, phase, p)
            copy = copy_to(ref, ref, gather_send.at[phase, s], gather_recv.at[phase, p], dev)
            copy.start()
            waits.append(copy)

        def arrived(p):
            ref = block(gathered, phase, p)
            copy_to(ref, ref, gather_send.at[phase, 0], gather_recv.at[phase, p], me).wait_recv()

        gathered[phase, pl.ds(pl.multiple_of(here * HEADS, HEADS), HEADS), :] = row32[
            ...
        ].astype(BF16)
        for k in range(1, chips):
            send_row(here, lax.rem(chip + k, chips) * 2 + core, k)
        send_row(here, sibling, 0)
        for k in range(1, chips):
            p = core * chips + lax.rem(chip + chips - k, chips)
            arrived(p)
            send_row(p, sibling, chips + k)
        for k in range(chips):
            arrived((1 - core) * chips + k)

        wide[...] = gathered[phase].astype(F32)
        for c in range(HEADS):
            rows[:, c * HDIM : (c + 1) * HDIM] = wide[pl.ds(c, n, stride=HEADS), :].astype(BF16)

        loaded(("down", phase))

        low = lax.dot_general(
            down[phase], rows[...], NT, preferred_element_type=F32
        ).T
        codes = jnp.where(mine, low, 0.0).astype(BF16)
        loaded(("up", phase))

        def raise_(k):
            cut = pl.ds(k * NSTEP, NSTEP)
            term = lax.dot_general(codes, up[phase, :, cut], NN, preferred_element_type=F32)
            first = k * (NSTEP // HDIM)
            half = first // HALF
            first = first - half * HALF + half * (n * HALF)
            for j in range(NSTEP // HDIM):
                wide[pl.ds(first + j, n, stride=HALF), :] = term[:, j * HDIM : (j + 1) * HDIM]

        side = chips * HALF
        to_pair = []
        for half in (0, 1):
            steps = width // NSTEP // 2
            for k in range(half * steps, (half + 1) * steps):
                raise_(k)
            own_delta[phase, half] = wide[half * n * HALF : (half + 1) * n * HALF, :].astype(BF16)
            copy = copy_to(
                own_delta.at[
                    phase, half, pl.ds(pl.multiple_of((1 - core) * side, side), side)
                ],
                sibling_delta.at[phase, half],
                pair_send.at[phase, half],
                pair_recv.at[phase, half],
                sibling,
            )
            copy.start()
            to_pair.append(copy)
            waits.append(copy)

        def piece(ref, half, c):
            return ref.at[phase, half, pl.ds(pl.multiple_of(c * HALF, HALF), HALF)]

        def forward(half):
            to_pair[half].wait_recv()
            pair_delta[phase, half] = (
                own_delta[
                    phase, half, pl.ds(pl.multiple_of(core * side, side), side), :
                ].astype(F32)
                + sibling_delta[phase, half].astype(F32)
            ).astype(BF16)
            for k in range(1, chips):
                other = lax.rem(chip + k, chips)
                copy = copy_to(
                    piece(pair_delta, half, other),
                    piece(delta_in, half, chip),
                    delta_send.at[phase, half, k],
                    delta_recv.at[phase, half, chip],
                    other * 2 + core,
                )
                copy.start()
                waits.append(copy)

        forward(0)

        def base_part(part, acc):
            loaded(("weight", phase, part))

            cut = pl.ds(part * depth, depth)
            return acc + lax.dot_general(
                rows[:, cut], weight[phase, cut, :], NN, preferred_element_type=F32
            )

        acc = jnp.zeros((n, cols), F32)
        for part in range(WPARTS // 2):
            acc = base_part(part, acc)
        forward(1)
        for part in range(WPARTS // 2, WPARTS):
            acc = base_part(part, acc)
        acc = acc.astype(BF16).astype(F32)
        for j in range(blocks):
            base_out[phase, pl.ds(j, n, stride=8), :] = acc[:, j * HDIM : (j + 1) * HDIM]

        def part_of(ref, p):
            return ref.at[phase, pl.ds(pl.multiple_of(p * 8, 8), 8)]

        for k in range(1, n):
            dev = lax.rem(me + k, n)
            p = lax.rem(dev, 2) * chips + lax.div(dev, 2)
            copy = copy_to(
                part_of(base_out, p),
                part_of(base_in, me),
                base_send.at[phase, k],
                base_recv.at[phase, me],
                dev,
            )
            copy.start()
            waits.append(copy)
        base_in[phase, pl.ds(pl.multiple_of(me * 8, 8), 8), :] = base_out[
            phase, pl.ds(pl.multiple_of(here * 8, 8), 8), :
        ]

        totals = []
        for half in (0, 1):
            total = pair_delta[
                phase, half, pl.ds(pl.multiple_of(chip * HALF, HALF), HALF), :
            ].astype(F32)
            for k in range(1, chips):
                other = lax.rem(chip + chips - k, chips)
                ref = piece(delta_in, half, other)
                copy_to(
                    ref, ref, delta_send.at[phase, half, 0], delta_recv.at[phase, half, other], me
                ).wait_recv()
                total = total + delta_in[
                    phase, half, pl.ds(pl.multiple_of(other * HALF, HALF), HALF), :
                ].astype(F32)
            totals.append(total)
        total = jnp.concatenate(totals, axis=0)
        for k in range(1, n):
            src = lax.rem(me + n - k, n)
            ref = part_of(base_in, src)
            copy_to(ref, ref, base_send.at[phase, 0], base_recv.at[phase, src], me).wait_recv()
        for src in range(n):
            row32[pl.ds(src * blocks, blocks), :] = base_in[phase, pl.ds(src * 8, blocks), :]
        result = (row32[...] + total).astype(BF16)
        for copy in waits:
            copy.wait_send()
        return result

    row32[...] = project(0).astype(F32)

    loaded("kv")
    cache_len = kv.shape[1]
    length = length_ref[0]
    scores = []
    for g in range(KVH):
        q = row32[pl.ds(g * GROUP, GROUP), :].astype(BF16)
        scores.append(
            lax.dot_general(
                q, kv[0, :, g * HDIM : (g + 1) * HDIM], NT, preferred_element_type=F32
            )
        )
    scores = jnp.concatenate(scores, axis=0) * SCALING
    visible = lax.broadcasted_iota(jnp.int32, (HEADS, cache_len), 1) < length
    masked = jnp.where(visible, scores, -1e30)
    highest = jnp.max(masked, axis=-1, keepdims=True)
    expon = jnp.where(visible, jnp.exp(masked - highest), 0.0)
    probs = expon / jnp.sum(expon, axis=-1, keepdims=True)
    for g in range(KVH):
        row32[pl.ds(g * GROUP, GROUP), :] = lax.dot_general(
            probs[g * GROUP : (g + 1) * GROUP].astype(BF16),
            kv[1, :, g * HDIM : (g + 1) * HDIM],
            NN,
            preferred_element_type=F32,
        )

    out_ref[...] = project(1)


WPARTS = 4
NSTEP = 512


def fused_body(
    hidden,
    query_weight,
    output_weight,
    adapter_down,
    adapter_up,
    kv_cache,
    cache_lengths,
    row_variant,
    variant_slot,
):
    n = lax.axis_size("dp")
    width = hidden.shape[1]
    owned, _, _, rank = adapter_down.shape
    cols = query_weight.shape[1]
    chips = n // 2
    vmem = pl.BlockSpec(memory_space=pltpu.VMEM)
    hbm = pl.BlockSpec(memory_space=pltpu.HBM)
    dma = pltpu.SemaphoreType.DMA
    weights = width * (2 * cols + 4 * owned * rank)
    macs = n * weights + 2 * HEADS * HDIM * kv_cache.shape[2]
    out = pl.pallas_call(
        functools.partial(attention_kernel, n),
        out_shape=jax.ShapeDtypeStruct((HEADS, HDIM), BF16),
        in_specs=[hbm] * 9,
        out_specs=vmem,
        scratch_shapes=[
            pltpu.SMEM(row_variant.shape, jnp.int32),
            pltpu.SMEM(variant_slot.shape, jnp.int32),
            pltpu.SMEM(cache_lengths.shape, jnp.int32),
            pltpu.VMEM(hidden.shape, BF16),
            pltpu.VMEM((2, width, cols), BF16),
            pltpu.VMEM((2, owned * rank, width), BF16),
            pltpu.VMEM((2, owned * rank, width), BF16),
            pltpu.VMEM(kv_cache.shape[1:], BF16),
            pltpu.VMEM((2, n * HEADS, HDIM), BF16),
            pltpu.VMEM((n * HEADS, HDIM), F32),
            pltpu.VMEM((n, width), BF16),
            pltpu.VMEM((HEADS, HDIM), F32),
            pltpu.VMEM((2, 2, n * HALF, HDIM), BF16),
            pltpu.VMEM((2, 2, chips * HALF, HDIM), BF16),
            pltpu.VMEM((2, 2, chips * HALF, HDIM), BF16),
            pltpu.VMEM((2, 2, chips * HALF, HDIM), BF16),
            pltpu.VMEM((2, n * 8, HDIM), F32),
            pltpu.VMEM((2, n * 8, HDIM), F32),
            dma((4 * owned + 2 * WPARTS + 5,)),
            dma((2, n)),
            dma((2, n)),
            dma((2, 2)),
            dma((2, 2)),
            dma((2, 2, chips)),
            dma((2, 2, chips)),
            dma((2, n)),
            dma((2, n)),
        ],
        compiler_params=pltpu.CompilerParams(
            collective_id=0, has_side_effects=True, vmem_limit_bytes=63 * MIB
        ),
        cost_estimate=pl.CostEstimate(
            flops=2 * macs,
            bytes_accessed=2 * (weights + kv_cache.size),
            transcendentals=HEADS * kv_cache.shape[2],
        ),
        name="adapter_attention",
    )(
        row_variant,
        variant_slot,
        cache_lengths,
        hidden,
        query_weight,
        output_weight,
        jnp.swapaxes(adapter_down, 2, 3),
        adapter_up,
        kv_cache,
    )
    return out.reshape(1, width)


def fits(mesh, hidden, query_weight, adapter_down, kv_cache):
    n = mesh.shape["dp"]
    cols = query_weight.shape[1] // n
    width = hidden.shape[1]
    owned = adapter_down.shape[0] // n
    held = 4 * width * cols + 8 * owned * adapter_down.shape[3] * width
    held += 2 * kv_cache.size // kv_cache.shape[0]
    return (
        hidden.shape[0] == n * mesh.shape["groups"]
        and width == HEADS * HDIM
        and n % 16 == 0
        and n <= 32
        and cols % HDIM == 0
        and cols <= 8 * HDIM
        and held <= 40 * MIB
    )


def body(
    hidden,
    query_weight,
    output_weight,
    adapter_down,
    adapter_up,
    kv_cache,
    cache_lengths,
    row_variant,
    variant_slot,
):
    devices = lax.axis_size("dp")
    myself = lax.axis_index("dp")
    owned = adapter_down.shape[0]
    rank_size = adapter_down.shape[3]
    width = hidden.shape[1]
    rows_dev = hidden.shape[0]
    all_rows = rows_dev * devices
    row_slot = jnp.sum(
        jnp.where(
            row_variant[:, None] == jnp.arange(variant_slot.shape[0], dtype=jnp.int32)[None, :],
            variant_slot[None, :],
            0,
        ),
        axis=1,
    )
    my_slots = myself * owned + jnp.arange(owned, dtype=jnp.int32)

    def project(row_block, weight, target):
        col_count = weight.shape[1]
        shard_rows = lax.all_gather(row_block, "dp", axis=0, tiled=True)
        base_part = jnp.dot(shard_rows, weight, preferred_element_type=jnp.float32)
        lowered = jnp.einsum(
            "pd,sdr->psr", shard_rows, adapter_down[:, target], preferred_element_type=jnp.float32
        )
        owner_mask = (row_slot[:, None] == my_slots[None, :]).astype(jnp.float32)
        reduced = jnp.sum(lowered * owner_mask[:, :, None], axis=1)
        joined = jnp.concatenate([base_part, reduced], axis=1)
        base_cols = joined[:, :col_count].astype(jnp.bfloat16)
        reduced = joined[:, col_count:]
        codes = reduced.astype(jnp.bfloat16)
        picked = (row_slot[:, None] == my_slots[None, :]).astype(jnp.bfloat16)
        spread = (picked[:, :, None] * codes[:, None, :]).reshape(all_rows, owned * rank_size)
        deltas = jnp.dot(
            spread,
            adapter_up[:, target].reshape(owned * rank_size, width),
            preferred_element_type=jnp.float32,
        ).astype(jnp.bfloat16)
        arrived = lax.all_to_all(base_cols, "dp", split_axis=0, concat_axis=1, tiled=True)
        returned = lax.all_to_all(
            deltas.reshape(all_rows, 1, width), "dp", split_axis=0, concat_axis=1, tiled=True
        )
        summed = jnp.sum(returned, axis=1, dtype=jnp.float32)
        return (arrived.astype(jnp.float32) + summed).astype(jnp.bfloat16)

    queries = project(hidden, query_weight, 0)
    cache_len = kv_cache.shape[2]
    grouped = queries.reshape(rows_dev, KVH, HEADS // KVH, HDIM)
    key_rows = kv_cache[:, 0].reshape(rows_dev, cache_len, KVH, HDIM)
    value_rows = kv_cache[:, 1].reshape(rows_dev, cache_len, KVH, HDIM)
    scaling = 1.0 / math.sqrt(HDIM)
    scores = (
        jnp.einsum("rkgd,rckd->rkgc", grouped, key_rows, preferred_element_type=jnp.float32)
        * scaling
    )
    visible = (jnp.arange(cache_len, dtype=jnp.int32)[None, :] < cache_lengths[:, None])[
        :, None, None, :
    ]
    masked = jnp.where(visible, scores, -1e30)
    highest = jnp.max(masked, axis=-1, keepdims=True)
    expon = jnp.where(visible, jnp.exp(masked - highest), 0.0)
    probs = (expon / jnp.sum(expon, axis=-1, keepdims=True)).astype(jnp.bfloat16)
    mixed = jnp.einsum("rkgc,rckd->rkgd", probs, value_rows, preferred_element_type=jnp.float32)
    mixed = mixed.astype(jnp.bfloat16).reshape(rows_dev, width)
    return project(mixed, output_weight, 1)


def solution(mesh):
    in_specs = (
        P(("groups", "dp"), None),
        P(None, "dp"),
        P(None, "dp"),
        P("dp", None, None, None),
        P("dp", None, None, None),
        P(("groups", "dp"), None, None, None),
        P(("groups", "dp")),
        P("groups"),
        P(),
    )

    def run(*args):
        fused = fits(mesh, args[0], args[1], args[3], args[5])
        return jax.shard_map(
            fused_body if fused else body,
            mesh=mesh,
            in_specs=in_specs,
            out_specs=P(("groups", "dp"), None),
            check_vma=False,
        )(*args)

    return run
```

```python
import functools
import math

import jax
import jax.numpy as jnp
from jax import lax
from jax.experimental import pallas as pl
from jax.experimental.pallas import tpu as pltpu
from jax.sharding import PartitionSpec as P

HEADS = 64
KVH = 8
HDIM = 128
GROUP = HEADS // KVH
HALF = HEADS // 2
F32 = jnp.float32
BF16 = jnp.bfloat16
SCALING = 1.0 / math.sqrt(HDIM)
MIB = 1 << 20
NN = (((1,), (0,)), ((), ()))
NT = (((1,), (1,)), ((), ()))


def attention_kernel(
    n,
    variant_hbm,
    slots_hbm,
    length_hbm,
    hidden_hbm,
    wq_hbm,
    wo_hbm,
    down_hbm,
    up_hbm,
    kv_hbm,
    out_ref,
    variant_ref,
    slots_ref,
    length_ref,
    hidden_ref,
    weight,
    down,
    up,
    kv,
    gathered,
    wide,
    rows,
    row32,
    own_delta,
    sibling_delta,
    pair_delta,
    delta_in,
    base_out,
    base_in,
    local_sem,
    gather_send,
    gather_recv,
    pair_send,
    pair_recv,
    delta_send,
    delta_recv,
    base_send,
    base_recv,
):
    chips = n // 2
    owned = down_hbm.shape[0]
    rank = down_hbm.shape[2]
    width = down_hbm.shape[3]
    cols = wq_hbm.shape[1]
    blocks = cols // HDIM
    me = lax.axis_index("dp")
    core = lax.rem(me, 2)
    chip = lax.div(me, 2)
    here = core * chips + chip

    def copy_to(src, dst, send, recv, dev):
        return pltpu.make_async_remote_copy(
            src_ref=src,
            dst_ref=dst,
            send_sem=send,
            recv_sem=recv,
            device_id={"dp": dev},
            device_id_type=pl.DeviceIdType.MESH,
        )

    depth = width // WPARTS
    loads = {}
    count = 0

    def load(name, src, dst):
        nonlocal count
        copy = pltpu.make_async_copy(src, dst, local_sem.at[count])
        count += 1
        copy.start()
        loads.setdefault(name, []).append(copy)

    load("hidden", hidden_hbm, hidden_ref)
    load("variant", variant_hbm, variant_ref)
    load("slots", slots_hbm, slots_ref)
    load("length", length_hbm, length_ref)
    for phase, w_hbm in ((0, wq_hbm), (1, wo_hbm)):
        for s in range(owned):
            load(("down", phase), down_hbm.at[s, phase], down.at[phase, pl.ds(s * rank, rank)])
        for s in range(owned):
            load(("up", phase), up_hbm.at[s, phase], up.at[phase, pl.ds(s * rank, rank)])
        for part in range(WPARTS):
            cut = pl.ds(part * depth, depth)
            load(("weight", phase, part), w_hbm.at[cut], weight.at[phase, cut])
        if phase == 0:
            load("kv", kv_hbm.at[0], kv)

    def loaded(name):
        for copy in loads[name]:
            copy.wait()

    barrier = pltpu.get_barrier_semaphore()
    for k in range(1, n):
        pl.semaphore_signal(
            barrier,
            inc=1,
            device_id={"dp": lax.rem(me + k, n)},
            device_id_type=pl.DeviceIdType.MESH,
        )

    loaded("hidden")
    for c in range(HEADS):
        row32[pl.ds(c, 1), :] = hidden_ref[:, c * HDIM : (c + 1) * HDIM].astype(F32)

    loaded("variant")
    loaded("slots")
    loaded("length")

    place = lax.broadcasted_iota(jnp.int32, (n, owned * rank), 0)
    lane_slot = me * owned + lax.div(
        lax.broadcasted_iota(jnp.int32, (n, owned * rank), 1), rank
    )
    row_slot = jnp.zeros((n, owned * rank), jnp.int32)
    for p in range(n):
        row = (p % chips) * 2 + p // chips
        row_slot = jnp.where(place == p, slots_ref[variant_ref[row]], row_slot)
    mine = row_slot == lane_slot

    pl.semaphore_wait(barrier, n - 1)

    def block(ref, phase, p):
        return ref.at[phase, pl.ds(pl.multiple_of(p * HEADS, HEADS), HEADS)]

    def project(phase):
        sibling = me + 1 - 2 * core
        waits = []

        def send_row(p, dev, s):
            ref = block(gathered, phase, p)
            copy = copy_to(ref, ref, gather_send.at[phase, s], gather_recv.at[phase, p], dev)
            copy.start()
            waits.append(copy)

        def arrived(p):
            ref = block(gathered, phase, p)
            copy_to(ref, ref, gather_send.at[phase, 0], gather_recv.at[phase, p], me).wait_recv()

        gathered[phase, pl.ds(pl.multiple_of(here * HEADS, HEADS), HEADS), :] = row32[
            ...
        ].astype(BF16)
        for k in range(1, chips):
            send_row(here, lax.rem(chip + k, chips) * 2 + core, k)
        send_row(here, sibling, 0)
        while late:
            late.pop().wait_send()
        for k in range(1, chips):
            p = core * chips + lax.rem(chip + chips - k, chips)
            arrived(p)
            send_row(p, sibling, chips + k)
        for k in range(chips):
            arrived((1 - core) * chips + k)

        wide[...] = gathered[phase].astype(F32)
        for c in range(HEADS):
            rows[:, c * HDIM : (c + 1) * HDIM] = wide[pl.ds(c, n, stride=HEADS), :].astype(BF16)

        loaded(("down", phase))

        low = lax.dot_general(
            down[phase], rows[...], NT, preferred_element_type=F32
        ).T
        codes = jnp.where(mine, low, 0.0).astype(BF16)
        loaded(("up", phase))

        def raise_(k):
            cut = pl.ds(k * NSTEP, NSTEP)
            term = lax.dot_general(codes, up[phase, :, cut], NN, preferred_element_type=F32)
            first = k * (NSTEP // HDIM)
            half = first // HALF
            first = first - half * HALF + half * (n * HALF)
            for j in range(NSTEP // HDIM):
                wide[pl.ds(first + j, n, stride=HALF), :] = term[:, j * HDIM : (j + 1) * HDIM]

        side = chips * HALF
        to_pair = []
        for half in (0, 1):
            steps = width // NSTEP // 2
            for k in range(half * steps, (half + 1) * steps):
                raise_(k)
            own_delta[phase, half] = wide[half * n * HALF : (half + 1) * n * HALF, :].astype(BF16)
            copy = copy_to(
                own_delta.at[
                    phase, half, pl.ds(pl.multiple_of((1 - core) * side, side), side)
                ],
                sibling_delta.at[phase, half],
                pair_send.at[phase, half],
                pair_recv.at[phase, half],
                sibling,
            )
            copy.start()
            to_pair.append(copy)
            waits.append(copy)

        def piece(ref, half, c):
            return ref.at[phase, half, pl.ds(pl.multiple_of(c * HALF, HALF), HALF)]

        def forward(half):
            to_pair[half].wait_recv()
            pair_delta[phase, half] = (
                own_delta[
                    phase, half, pl.ds(pl.multiple_of(core * side, side), side), :
                ].astype(F32)
                + sibling_delta[phase, half].astype(F32)
            ).astype(BF16)
            for k in range(1, chips):
                other = lax.rem(chip + k, chips)
                copy = copy_to(
                    piece(pair_delta, half, other),
                    piece(delta_in, half, chip),
                    delta_send.at[phase, half, k],
                    delta_recv.at[phase, half, chip],
                    other * 2 + core,
                )
                copy.start()
                waits.append(copy)

        forward(0)

        def base_part(part, acc):
            loaded(("weight", phase, part))

            cut = pl.ds(part * depth, depth)
            return acc + lax.dot_general(
                rows[:, cut], weight[phase, cut, :], NN, preferred_element_type=F32
            )

        acc = jnp.zeros((n, cols), F32)
        for part in range(WPARTS // 2):
            acc = base_part(part, acc)
        forward(1)
        for part in range(WPARTS // 2, WPARTS):
            acc = base_part(part, acc)
        acc = acc.astype(BF16).astype(F32)
        for j in range(blocks):
            base_out[phase, pl.ds(j, n, stride=8), :] = acc[:, j * HDIM : (j + 1) * HDIM]

        def part_of(ref, p):
            return ref.at[phase, pl.ds(pl.multiple_of(p * 8, 8), 8)]

        for k in range(1, n):
            dev = lax.rem(me + k, n)
            p = lax.rem(dev, 2) * chips + lax.div(dev, 2)
            copy = copy_to(
                part_of(base_out, p),
                part_of(base_in, me),
                base_send.at[phase, k],
                base_recv.at[phase, me],
                dev,
            )
            copy.start()
            late.append(copy)
        base_in[phase, pl.ds(pl.multiple_of(me * 8, 8), 8), :] = base_out[
            phase, pl.ds(pl.multiple_of(here * 8, 8), 8), :
        ]

        for copy in waits:
            copy.wait_send()
        totals = []
        for half in (0, 1):
            total = pair_delta[
                phase, half, pl.ds(pl.multiple_of(chip * HALF, HALF), HALF), :
            ].astype(F32)
            for k in range(1, chips):
                other = lax.rem(chip + chips - k, chips)
                ref = piece(delta_in, half, other)
                copy_to(
                    ref, ref, delta_send.at[phase, half, 0], delta_recv.at[phase, half, other], me
                ).wait_recv()
                total = total + delta_in[
                    phase, half, pl.ds(pl.multiple_of(other * HALF, HALF), HALF), :
                ].astype(F32)
            totals.append(total)
        total = jnp.concatenate(totals, axis=0)
        for k in range(1, n):
            src = lax.rem(me + n - k, n)
            ref = part_of(base_in, src)
            copy_to(ref, ref, base_send.at[phase, 0], base_recv.at[phase, src], me).wait_recv()
        for src in range(n):
            row32[pl.ds(src * blocks, blocks), :] = base_in[phase, pl.ds(src * 8, blocks), :]
        result = (row32[...] + total).astype(BF16)
        return result

    late = []
    row32[...] = project(0).astype(F32)

    loaded("kv")
    cache_len = kv.shape[1]
    length = length_ref[0]
    scores = []
    for g in range(KVH):
        q = row32[pl.ds(g * GROUP, GROUP), :].astype(BF16)
        scores.append(
            lax.dot_general(
                q, kv[0, :, g * HDIM : (g + 1) * HDIM], NT, preferred_element_type=F32
            )
        )
    scores = jnp.concatenate(scores, axis=0) * SCALING
    visible = lax.broadcasted_iota(jnp.int32, (HEADS, cache_len), 1) < length
    masked = jnp.where(visible, scores, -1e30)
    highest = jnp.max(masked, axis=-1, keepdims=True)
    expon = jnp.where(visible, jnp.exp(masked - highest), 0.0)
    probs = expon / jnp.sum(expon, axis=-1, keepdims=True)
    for g in range(KVH):
        row32[pl.ds(g * GROUP, GROUP), :] = lax.dot_general(
            probs[g * GROUP : (g + 1) * GROUP].astype(BF16),
            kv[1, :, g * HDIM : (g + 1) * HDIM],
            NN,
            preferred_element_type=F32,
        )

    out_ref[...] = project(1)
    for copy in late:
        copy.wait_send()


WPARTS = 4
NSTEP = 512


def fused_body(
    hidden,
    query_weight,
    output_weight,
    adapter_down,
    adapter_up,
    kv_cache,
    cache_lengths,
    row_variant,
    variant_slot,
):
    n = lax.axis_size("dp")
    width = hidden.shape[1]
    owned, _, _, rank = adapter_down.shape
    cols = query_weight.shape[1]
    chips = n // 2
    vmem = pl.BlockSpec(memory_space=pltpu.VMEM)
    hbm = pl.BlockSpec(memory_space=pltpu.HBM)
    dma = pltpu.SemaphoreType.DMA
    weights = width * (2 * cols + 4 * owned * rank)
    macs = n * weights + 2 * HEADS * HDIM * kv_cache.shape[2]
    out = pl.pallas_call(
        functools.partial(attention_kernel, n),
        out_shape=jax.ShapeDtypeStruct((HEADS, HDIM), BF16),
        in_specs=[hbm] * 9,
        out_specs=vmem,
        scratch_shapes=[
            pltpu.SMEM(row_variant.shape, jnp.int32),
            pltpu.SMEM(variant_slot.shape, jnp.int32),
            pltpu.SMEM(cache_lengths.shape, jnp.int32),
            pltpu.VMEM(hidden.shape, BF16),
            pltpu.VMEM((2, width, cols), BF16),
            pltpu.VMEM((2, owned * rank, width), BF16),
            pltpu.VMEM((2, owned * rank, width), BF16),
            pltpu.VMEM(kv_cache.shape[1:], BF16),
            pltpu.VMEM((2, n * HEADS, HDIM), BF16),
            pltpu.VMEM((n * HEADS, HDIM), F32),
            pltpu.VMEM((n, width), BF16),
            pltpu.VMEM((HEADS, HDIM), F32),
            pltpu.VMEM((2, 2, n * HALF, HDIM), BF16),
            pltpu.VMEM((2, 2, chips * HALF, HDIM), BF16),
            pltpu.VMEM((2, 2, chips * HALF, HDIM), BF16),
            pltpu.VMEM((2, 2, chips * HALF, HDIM), BF16),
            pltpu.VMEM((2, n * 8, HDIM), F32),
            pltpu.VMEM((2, n * 8, HDIM), F32),
            dma((4 * owned + 2 * WPARTS + 5,)),
            dma((2, n)),
            dma((2, n)),
            dma((2, 2)),
            dma((2, 2)),
            dma((2, 2, chips)),
            dma((2, 2, chips)),
            dma((2, n)),
            dma((2, n)),
        ],
        compiler_params=pltpu.CompilerParams(
            collective_id=0, has_side_effects=True, vmem_limit_bytes=63 * MIB
        ),
        cost_estimate=pl.CostEstimate(
            flops=2 * macs,
            bytes_accessed=2 * (weights + kv_cache.size),
            transcendentals=HEADS * kv_cache.shape[2],
        ),
        name="adapter_attention",
    )(
        row_variant,
        variant_slot,
        cache_lengths,
        hidden,
        query_weight,
        output_weight,
        jnp.swapaxes(adapter_down, 2, 3),
        adapter_up,
        kv_cache,
    )
    return out.reshape(1, width)


def fits(mesh, hidden, query_weight, adapter_down, kv_cache):
    n = mesh.shape["dp"]
    cols = query_weight.shape[1] // n
    width = hidden.shape[1]
    owned = adapter_down.shape[0] // n
    held = 4 * width * cols + 8 * owned * adapter_down.shape[3] * width
    held += 2 * kv_cache.size // kv_cache.shape[0]
    return (
        hidden.shape[0] == n * mesh.shape["groups"]
        and width == HEADS * HDIM
        and n % 16 == 0
        and n <= 32
        and cols % HDIM == 0
        and cols <= 8 * HDIM
        and held <= 40 * MIB
    )


def body(
    hidden,
    query_weight,
    output_weight,
    adapter_down,
    adapter_up,
    kv_cache,
    cache_lengths,
    row_variant,
    variant_slot,
):
    devices = lax.axis_size("dp")
    myself = lax.axis_index("dp")
    owned = adapter_down.shape[0]
    rank_size = adapter_down.shape[3]
    width = hidden.shape[1]
    rows_dev = hidden.shape[0]
    all_rows = rows_dev * devices
    row_slot = jnp.sum(
        jnp.where(
            row_variant[:, None] == jnp.arange(variant_slot.shape[0], dtype=jnp.int32)[None, :],
            variant_slot[None, :],
            0,
        ),
        axis=1,
    )
    my_slots = myself * owned + jnp.arange(owned, dtype=jnp.int32)

    def project(row_block, weight, target):
        col_count = weight.shape[1]
        shard_rows = lax.all_gather(row_block, "dp", axis=0, tiled=True)
        base_part = jnp.dot(shard_rows, weight, preferred_element_type=jnp.float32)
        lowered = jnp.einsum(
            "pd,sdr->psr", shard_rows, adapter_down[:, target], preferred_element_type=jnp.float32
        )
        owner_mask = (row_slot[:, None] == my_slots[None, :]).astype(jnp.float32)
        reduced = jnp.sum(lowered * owner_mask[:, :, None], axis=1)
        joined = jnp.concatenate([base_part, reduced], axis=1)
        base_cols = joined[:, :col_count].astype(jnp.bfloat16)
        reduced = joined[:, col_count:]
        codes = reduced.astype(jnp.bfloat16)
        picked = (row_slot[:, None] == my_slots[None, :]).astype(jnp.bfloat16)
        spread = (picked[:, :, None] * codes[:, None, :]).reshape(all_rows, owned * rank_size)
        deltas = jnp.dot(
            spread,
            adapter_up[:, target].reshape(owned * rank_size, width),
            preferred_element_type=jnp.float32,
        ).astype(jnp.bfloat16)
        arrived = lax.all_to_all(base_cols, "dp", split_axis=0, concat_axis=1, tiled=True)
        returned = lax.all_to_all(
            deltas.reshape(all_rows, 1, width), "dp", split_axis=0, concat_axis=1, tiled=True
        )
        summed = jnp.sum(returned, axis=1, dtype=jnp.float32)
        return (arrived.astype(jnp.float32) + summed).astype(jnp.bfloat16)

    queries = project(hidden, query_weight, 0)
    cache_len = kv_cache.shape[2]
    grouped = queries.reshape(rows_dev, KVH, HEADS // KVH, HDIM)
    key_rows = kv_cache[:, 0].reshape(rows_dev, cache_len, KVH, HDIM)
    value_rows = kv_cache[:, 1].reshape(rows_dev, cache_len, KVH, HDIM)
    scaling = 1.0 / math.sqrt(HDIM)
    scores = (
        jnp.einsum("rkgd,rckd->rkgc", grouped, key_rows, preferred_element_type=jnp.float32)
        * scaling
    )
    visible = (jnp.arange(cache_len, dtype=jnp.int32)[None, :] < cache_lengths[:, None])[
        :, None, None, :
    ]
    masked = jnp.where(visible, scores, -1e30)
    highest = jnp.max(masked, axis=-1, keepdims=True)
    expon = jnp.where(visible, jnp.exp(masked - highest), 0.0)
    probs = (expon / jnp.sum(expon, axis=-1, keepdims=True)).astype(jnp.bfloat16)
    mixed = jnp.einsum("rkgc,rckd->rkgd", probs, value_rows, preferred_element_type=jnp.float32)
    mixed = mixed.astype(jnp.bfloat16).reshape(rows_dev, width)
    return project(mixed, output_weight, 1)


def solution(mesh):
    in_specs = (
        P(("groups", "dp"), None),
        P(None, "dp"),
        P(None, "dp"),
        P("dp", None, None, None),
        P("dp", None, None, None),
        P(("groups", "dp"), None, None, None),
        P(("groups", "dp")),
        P("groups"),
        P(),
    )

    def run(*args):
        fused = fits(mesh, args[0], args[1], args[3], args[5])
        return jax.shard_map(
            fused_body if fused else body,
            mesh=mesh,
            in_specs=in_specs,
            out_specs=P(("groups", "dp"), None),
            check_vma=False,
        )(*args)

    return run
```

```python
import functools
import math

import jax
import jax.numpy as jnp
from jax import lax
from jax.experimental import pallas as pl
from jax.experimental.pallas import tpu as pltpu
from jax.sharding import PartitionSpec as P

HEADS = 64
KVH = 8
HDIM = 128
GROUP = HEADS // KVH
HALF = HEADS // 2
F32 = jnp.float32
BF16 = jnp.bfloat16
SCALING = 1.0 / math.sqrt(HDIM)
MIB = 1 << 20
NN = (((1,), (0,)), ((), ()))
NT = (((1,), (1,)), ((), ()))


def attention_kernel(
    n,
    variant_hbm,
    slots_hbm,
    length_hbm,
    hidden_hbm,
    wq_hbm,
    wo_hbm,
    down_hbm,
    up_hbm,
    kv_hbm,
    out_ref,
    variant_ref,
    slots_ref,
    length_ref,
    hidden_ref,
    weight,
    down,
    up,
    kv,
    gathered,
    wide,
    rows,
    row32,
    own_delta,
    sibling_delta,
    pair_delta,
    delta_in,
    base_out,
    base_in,
    local_sem,
    gather_send,
    gather_recv,
    pair_send,
    pair_recv,
    delta_send,
    delta_recv,
    base_send,
    base_recv,
):
    chips = n // 2
    owned = down_hbm.shape[0]
    rank = down_hbm.shape[2]
    width = down_hbm.shape[3]
    cols = wq_hbm.shape[1]
    blocks = cols // HDIM
    me = lax.axis_index("dp")
    core = lax.rem(me, 2)
    chip = lax.div(me, 2)
    here = core * chips + chip

    def copy_to(src, dst, send, recv, dev):
        return pltpu.make_async_remote_copy(
            src_ref=src,
            dst_ref=dst,
            send_sem=send,
            recv_sem=recv,
            device_id={"dp": dev},
            device_id_type=pl.DeviceIdType.MESH,
        )

    depth = width // WPARTS
    loads = {}
    count = 0

    def load(name, src, dst):
        nonlocal count
        copy = pltpu.make_async_copy(src, dst, local_sem.at[count])
        count += 1
        copy.start()
        loads.setdefault(name, []).append(copy)

    load("hidden", hidden_hbm, hidden_ref)
    load("variant", variant_hbm, variant_ref)
    load("slots", slots_hbm, slots_ref)
    load("length", length_hbm, length_ref)
    for phase, w_hbm in ((0, wq_hbm), (1, wo_hbm)):
        for s in range(owned):
            load(("down", phase), down_hbm.at[s, phase], down.at[phase, pl.ds(s * rank, rank)])
        for s in range(owned):
            load(("up", phase), up_hbm.at[s, phase], up.at[phase, pl.ds(s * rank, rank)])
        for part in range(WPARTS):
            cut = pl.ds(part * depth, depth)
            load(("weight", phase, part), w_hbm.at[cut], weight.at[phase, cut])
        if phase == 0:
            load("kv", kv_hbm.at[0], kv)

    def loaded(name):
        for copy in loads[name]:
            copy.wait()

    barrier = pltpu.get_barrier_semaphore()
    for k in range(1, n):
        pl.semaphore_signal(
            barrier,
            inc=1,
            device_id={"dp": lax.rem(me + k, n)},
            device_id_type=pl.DeviceIdType.MESH,
        )

    loaded("hidden")
    for c in range(HEADS):
        row32[pl.ds(c, 1), :] = hidden_ref[:, c * HDIM : (c + 1) * HDIM].astype(F32)

    loaded("variant")
    loaded("slots")
    loaded("length")

    place = lax.broadcasted_iota(jnp.int32, (n, owned * rank), 0)
    lane_slot = me * owned + lax.div(
        lax.broadcasted_iota(jnp.int32, (n, owned * rank), 1), rank
    )
    row_slot = jnp.zeros((n, owned * rank), jnp.int32)
    for p in range(n):
        row = (p % chips) * 2 + p // chips
        row_slot = jnp.where(place == p, slots_ref[variant_ref[row]], row_slot)
    mine = row_slot == lane_slot

    pl.semaphore_wait(barrier, n - 1)

    def block(ref, phase, p):
        return ref.at[phase, pl.ds(pl.multiple_of(p * HEADS, HEADS), HEADS)]

    def project(phase):
        sibling = me + 1 - 2 * core
        waits = []

        def send_row(p, dev, s):
            ref = block(gathered, phase, p)
            copy = copy_to(ref, ref, gather_send.at[phase, s], gather_recv.at[phase, p], dev)
            copy.start()
            waits.append(copy)

        def arrived(p):
            ref = block(gathered, phase, p)
            copy_to(ref, ref, gather_send.at[phase, 0], gather_recv.at[phase, p], me).wait_recv()

        gathered[phase, pl.ds(pl.multiple_of(here * HEADS, HEADS), HEADS), :] = row32[
            ...
        ].astype(BF16)
        for k in range(1, chips):
            send_row(here, lax.rem(chip + k, chips) * 2 + core, k)
        send_row(here, sibling, 0)
        while late:
            late.pop().wait_send()
        for k in range(1, chips):
            p = core * chips + lax.rem(chip + chips - k, chips)
            arrived(p)
            send_row(p, sibling, chips + k)
        for k in range(chips):
            arrived((1 - core) * chips + k)

        wide[...] = gathered[phase].astype(F32)
        for c in range(HEADS):
            rows[:, c * HDIM : (c + 1) * HDIM] = wide[pl.ds(c, n, stride=HEADS), :].astype(BF16)

        loaded(("down", phase))

        low = lax.dot_general(
            down[phase], rows[...], NT, preferred_element_type=F32
        ).T
        codes = jnp.where(mine, low, 0.0).astype(BF16)
        loaded(("up", phase))

        def raise_(k):
            cut = pl.ds(k * NSTEP, NSTEP)
            term = lax.dot_general(codes, up[phase, :, cut], NN, preferred_element_type=F32)
            first = k * (NSTEP // HDIM)
            half = first // HALF
            first = first - half * HALF + half * (n * HALF)
            for j in range(NSTEP // HDIM):
                wide[pl.ds(first + j, n, stride=HALF), :] = term[:, j * HDIM : (j + 1) * HDIM]

        side = chips * HALF
        to_pair = []
        for half in (0, 1):
            steps = width // NSTEP // 2
            for k in range(half * steps, (half + 1) * steps):
                raise_(k)
            own_delta[phase, half] = wide[half * n * HALF : (half + 1) * n * HALF, :].astype(BF16)
            copy = copy_to(
                own_delta.at[
                    phase, half, pl.ds(pl.multiple_of((1 - core) * side, side), side)
                ],
                sibling_delta.at[phase, half],
                pair_send.at[phase, half],
                pair_recv.at[phase, half],
                sibling,
            )
            copy.start()
            to_pair.append(copy)
            waits.append(copy)

        def piece(ref, half, c):
            return ref.at[phase, half, pl.ds(pl.multiple_of(c * HALF, HALF), HALF)]

        def forward(half):
            to_pair[half].wait_recv()
            pair_delta[phase, half] = (
                own_delta[
                    phase, half, pl.ds(pl.multiple_of(core * side, side), side), :
                ].astype(F32)
                + sibling_delta[phase, half].astype(F32)
            ).astype(BF16)
            for k in range(1, chips):
                other = lax.rem(chip + k, chips)
                copy = copy_to(
                    piece(pair_delta, half, other),
                    piece(delta_in, half, chip),
                    delta_send.at[phase, half, k],
                    delta_recv.at[phase, half, chip],
                    other * 2 + core,
                )
                copy.start()
                waits.append(copy)

        forward(0)

        def base_part(part, acc):
            loaded(("weight", phase, part))

            cut = pl.ds(part * depth, depth)
            return acc + lax.dot_general(
                rows[:, cut], weight[phase, cut, :], NN, preferred_element_type=F32
            )

        acc = jnp.zeros((n, cols), F32)
        for part in range(1):
            acc = base_part(part, acc)
        forward(1)
        for part in range(1, WPARTS):
            acc = base_part(part, acc)
        acc = acc.astype(BF16).astype(F32)
        for j in range(blocks):
            base_out[phase, pl.ds(j, n, stride=8), :] = acc[:, j * HDIM : (j + 1) * HDIM]

        def part_of(ref, p):
            return ref.at[phase, pl.ds(pl.multiple_of(p * 8, 8), 8)]

        for k in range(1, n):
            dev = lax.rem(me + k, n)
            p = lax.rem(dev, 2) * chips + lax.div(dev, 2)
            copy = copy_to(
                part_of(base_out, p),
                part_of(base_in, me),
                base_send.at[phase, k],
                base_recv.at[phase, me],
                dev,
            )
            copy.start()
            late.append(copy)
        base_in[phase, pl.ds(pl.multiple_of(me * 8, 8), 8), :] = base_out[
            phase, pl.ds(pl.multiple_of(here * 8, 8), 8), :
        ]

        for copy in waits:
            copy.wait_send()
        totals = []
        for half in (0, 1):
            total = pair_delta[
                phase, half, pl.ds(pl.multiple_of(chip * HALF, HALF), HALF), :
            ].astype(F32)
            for k in range(1, chips):
                other = lax.rem(chip + chips - k, chips)
                ref = piece(delta_in, half, other)
                copy_to(
                    ref, ref, delta_send.at[phase, half, 0], delta_recv.at[phase, half, other], me
                ).wait_recv()
                total = total + delta_in[
                    phase, half, pl.ds(pl.multiple_of(other * HALF, HALF), HALF), :
                ].astype(F32)
            totals.append(total)
        total = jnp.concatenate(totals, axis=0)
        for k in range(1, n):
            src = lax.rem(me + n - k, n)
            ref = part_of(base_in, src)
            copy_to(ref, ref, base_send.at[phase, 0], base_recv.at[phase, src], me).wait_recv()
        for src in range(n):
            row32[pl.ds(src * blocks, blocks), :] = base_in[phase, pl.ds(src * 8, blocks), :]
        result = (row32[...] + total).astype(BF16)
        return result

    late = []
    row32[...] = project(0).astype(F32)

    loaded("kv")
    cache_len = kv.shape[1]
    length = length_ref[0]
    scores = []
    for g in range(KVH):
        q = row32[pl.ds(g * GROUP, GROUP), :].astype(BF16)
        scores.append(
            lax.dot_general(
                q, kv[0, :, g * HDIM : (g + 1) * HDIM], NT, preferred_element_type=F32
            )
        )
    scores = jnp.concatenate(scores, axis=0) * SCALING
    visible = lax.broadcasted_iota(jnp.int32, (HEADS, cache_len), 1) < length
    masked = jnp.where(visible, scores, -1e30)
    highest = jnp.max(masked, axis=-1, keepdims=True)
    expon = jnp.where(visible, jnp.exp(masked - highest), 0.0)
    probs = expon / jnp.sum(expon, axis=-1, keepdims=True)
    for g in range(KVH):
        row32[pl.ds(g * GROUP, GROUP), :] = lax.dot_general(
            probs[g * GROUP : (g + 1) * GROUP].astype(BF16),
            kv[1, :, g * HDIM : (g + 1) * HDIM],
            NN,
            preferred_element_type=F32,
        )

    out_ref[...] = project(1)
    for copy in late:
        copy.wait_send()


WPARTS = 4
NSTEP = 512


def fused_body(
    hidden,
    query_weight,
    output_weight,
    adapter_down,
    adapter_up,
    kv_cache,
    cache_lengths,
    row_variant,
    variant_slot,
):
    n = lax.axis_size("dp")
    width = hidden.shape[1]
    owned, _, _, rank = adapter_down.shape
    cols = query_weight.shape[1]
    chips = n // 2
    vmem = pl.BlockSpec(memory_space=pltpu.VMEM)
    hbm = pl.BlockSpec(memory_space=pltpu.HBM)
    dma = pltpu.SemaphoreType.DMA
    weights = width * (2 * cols + 4 * owned * rank)
    macs = n * weights + 2 * HEADS * HDIM * kv_cache.shape[2]
    out = pl.pallas_call(
        functools.partial(attention_kernel, n),
        out_shape=jax.ShapeDtypeStruct((HEADS, HDIM), BF16),
        in_specs=[hbm] * 9,
        out_specs=vmem,
        scratch_shapes=[
            pltpu.SMEM(row_variant.shape, jnp.int32),
            pltpu.SMEM(variant_slot.shape, jnp.int32),
            pltpu.SMEM(cache_lengths.shape, jnp.int32),
            pltpu.VMEM(hidden.shape, BF16),
            pltpu.VMEM((2, width, cols), BF16),
            pltpu.VMEM((2, owned * rank, width), BF16),
            pltpu.VMEM((2, owned * rank, width), BF16),
            pltpu.VMEM(kv_cache.shape[1:], BF16),
            pltpu.VMEM((2, n * HEADS, HDIM), BF16),
            pltpu.VMEM((n * HEADS, HDIM), F32),
            pltpu.VMEM((n, width), BF16),
            pltpu.VMEM((HEADS, HDIM), F32),
            pltpu.VMEM((2, 2, n * HALF, HDIM), BF16),
            pltpu.VMEM((2, 2, chips * HALF, HDIM), BF16),
            pltpu.VMEM((2, 2, chips * HALF, HDIM), BF16),
            pltpu.VMEM((2, 2, chips * HALF, HDIM), BF16),
            pltpu.VMEM((2, n * 8, HDIM), F32),
            pltpu.VMEM((2, n * 8, HDIM), F32),
            dma((4 * owned + 2 * WPARTS + 5,)),
            dma((2, n)),
            dma((2, n)),
            dma((2, 2)),
            dma((2, 2)),
            dma((2, 2, chips)),
            dma((2, 2, chips)),
            dma((2, n)),
            dma((2, n)),
        ],
        compiler_params=pltpu.CompilerParams(
            collective_id=0, has_side_effects=True, vmem_limit_bytes=63 * MIB
        ),
        cost_estimate=pl.CostEstimate(
            flops=2 * macs,
            bytes_accessed=2 * (weights + kv_cache.size),
            transcendentals=HEADS * kv_cache.shape[2],
        ),
        name="adapter_attention",
    )(
        row_variant,
        variant_slot,
        cache_lengths,
        hidden,
        query_weight,
        output_weight,
        jnp.swapaxes(adapter_down, 2, 3),
        adapter_up,
        kv_cache,
    )
    return out.reshape(1, width)


def fits(mesh, hidden, query_weight, adapter_down, kv_cache):
    n = mesh.shape["dp"]
    cols = query_weight.shape[1] // n
    width = hidden.shape[1]
    owned = adapter_down.shape[0] // n
    held = 4 * width * cols + 8 * owned * adapter_down.shape[3] * width
    held += 2 * kv_cache.size // kv_cache.shape[0]
    return (
        hidden.shape[0] == n * mesh.shape["groups"]
        and width == HEADS * HDIM
        and n % 16 == 0
        and n <= 32
        and cols % HDIM == 0
        and cols <= 8 * HDIM
        and held <= 40 * MIB
    )


def body(
    hidden,
    query_weight,
    output_weight,
    adapter_down,
    adapter_up,
    kv_cache,
    cache_lengths,
    row_variant,
    variant_slot,
):
    devices = lax.axis_size("dp")
    myself = lax.axis_index("dp")
    owned = adapter_down.shape[0]
    rank_size = adapter_down.shape[3]
    width = hidden.shape[1]
    rows_dev = hidden.shape[0]
    all_rows = rows_dev * devices
    row_slot = jnp.sum(
        jnp.where(
            row_variant[:, None] == jnp.arange(variant_slot.shape[0], dtype=jnp.int32)[None, :],
            variant_slot[None, :],
            0,
        ),
        axis=1,
    )
    my_slots = myself * owned + jnp.arange(owned, dtype=jnp.int32)

    def project(row_block, weight, target):
        col_count = weight.shape[1]
        shard_rows = lax.all_gather(row_block, "dp", axis=0, tiled=True)
        base_part = jnp.dot(shard_rows, weight, preferred_element_type=jnp.float32)
        lowered = jnp.einsum(
            "pd,sdr->psr", shard_rows, adapter_down[:, target], preferred_element_type=jnp.float32
        )
        owner_mask = (row_slot[:, None] == my_slots[None, :]).astype(jnp.float32)
        reduced = jnp.sum(lowered * owner_mask[:, :, None], axis=1)
        joined = jnp.concatenate([base_part, reduced], axis=1)
        base_cols = joined[:, :col_count].astype(jnp.bfloat16)
        reduced = joined[:, col_count:]
        codes = reduced.astype(jnp.bfloat16)
        picked = (row_slot[:, None] == my_slots[None, :]).astype(jnp.bfloat16)
        spread = (picked[:, :, None] * codes[:, None, :]).reshape(all_rows, owned * rank_size)
        deltas = jnp.dot(
            spread,
            adapter_up[:, target].reshape(owned * rank_size, width),
            preferred_element_type=jnp.float32,
        ).astype(jnp.bfloat16)
        arrived = lax.all_to_all(base_cols, "dp", split_axis=0, concat_axis=1, tiled=True)
        returned = lax.all_to_all(
            deltas.reshape(all_rows, 1, width), "dp", split_axis=0, concat_axis=1, tiled=True
        )
        summed = jnp.sum(returned, axis=1, dtype=jnp.float32)
        return (arrived.astype(jnp.float32) + summed).astype(jnp.bfloat16)

    queries = project(hidden, query_weight, 0)
    cache_len = kv_cache.shape[2]
    grouped = queries.reshape(rows_dev, KVH, HEADS // KVH, HDIM)
    key_rows = kv_cache[:, 0].reshape(rows_dev, cache_len, KVH, HDIM)
    value_rows = kv_cache[:, 1].reshape(rows_dev, cache_len, KVH, HDIM)
    scaling = 1.0 / math.sqrt(HDIM)
    scores = (
        jnp.einsum("rkgd,rckd->rkgc", grouped, key_rows, preferred_element_type=jnp.float32)
        * scaling
    )
    visible = (jnp.arange(cache_len, dtype=jnp.int32)[None, :] < cache_lengths[:, None])[
        :, None, None, :
    ]
    masked = jnp.where(visible, scores, -1e30)
    highest = jnp.max(masked, axis=-1, keepdims=True)
    expon = jnp.where(visible, jnp.exp(masked - highest), 0.0)
    probs = (expon / jnp.sum(expon, axis=-1, keepdims=True)).astype(jnp.bfloat16)
    mixed = jnp.einsum("rkgc,rckd->rkgd", probs, value_rows, preferred_element_type=jnp.float32)
    mixed = mixed.astype(jnp.bfloat16).reshape(rows_dev, width)
    return project(mixed, output_weight, 1)


def solution(mesh):
    in_specs = (
        P(("groups", "dp"), None),
        P(None, "dp"),
        P(None, "dp"),
        P("dp", None, None, None),
        P("dp", None, None, None),
        P(("groups", "dp"), None, None, None),
        P(("groups", "dp")),
        P("groups"),
        P(),
    )

    def run(*args):
        fused = fits(mesh, args[0], args[1], args[3], args[5])
        return jax.shard_map(
            fused_body if fused else body,
            mesh=mesh,
            in_specs=in_specs,
            out_specs=P(("groups", "dp"), None),
            check_vma=False,
        )(*args)

    return run
```
